32 devices in a mesh: space: 8 (over y, x, core), dp: 4 (over z).
Axes of the slice: x: 2, y: 2, z: 4, core: 2. Of those that a mesh axis runs over, the one named last changes fastest.
Arguments:
- volume: bfloat16 [256, 96, 8, 128], P(('dp', 'space')), parts along dimension 0, may hold values from -6 to 6
- kernel: bfloat16 [96, 2592], replicated, may hold values from -0.125 to 0.125
- beta: float32 [96], replicated, may hold values from 0.5 to 2
- gamma: float32 [96, 96], replicated, may hold values from 0 to 0.04
- cotangent: bfloat16 [32, 96, 8, 128], P(('dp', 'space')), parts along dimension 0, may hold values from -6 to 6
Outputs:
- normalized: bfloat16 [32, 96, 8, 128], P(('dp', 'space')), parts along dimension 0
- volume_input_gradient: bfloat16 [256, 96, 8, 128], P(('dp', 'space')), parts along dimension 0
- kernel_grad: float32 [384, 2592], P('dp'), parts along dimension 0
- gamma_grad: float32 [384, 96], P('dp'), parts along dimension 0
- beta_grad: float32 [384], P('dp'), parts along dimension 0
The draws below stay inside these ranges and needn't reach their ends.
There are 4 independent parts, one for each index of `dp`. The reference program is written for one: setup_inputs(seed, part) draws one part's arguments, and reference() takes and returns one part's arrays. A program takes and returns all parts, laid end to end along the dimension named above; an argument that names none is the same for every part. Nothing has to cross between parts.
All inputs are finite; a program needn't handle non-finite values.
Results may differ from the reference program's by a relative error of at most 0.0049.
Values may be sent and summed in bfloat16 or wider, within the bound.
A program may use at most 64 MiB of HBM per device.

```python
import math
import jax
import jax.numpy as jnp
from jax import lax

C = 96
BLOCK_INPUT_X = 16
BLOCK_INPUT_Y = 16
BLOCK_INPUT_Z = 32
BLOCK_OUTPUT_X = 8
BLOCK_OUTPUT_Y = 8
BLOCK_OUTPUT_Z = 16
CELLS = 8192
N_SPACE = 8


def level_of(rng, dims, shards, smallest, high):
    factor_of, own = 1.0, jax.random.fold_in(rng, 6)
    for dim, blocks in shards:
        draws = jnp.exp(jax.random.uniform(jax.random.fold_in(own, dim), (blocks,), jnp.float32, smallest / len(shards), high / len(shards)))
        factor_of = factor_of * jnp.repeat(draws, dims[dim] // blocks).reshape([-1 if axis == dim else 1 for axis in range(len(dims))])
    return factor_of


def scatter_about(key, extent, spread, limit, shards=(), kind=jnp.bfloat16):
    drawn = jax.random.normal(key, extent, jnp.float32) * spread
    if len(shards) > 0:
        drawn = level_of(key, extent, shards, -0.22, 0.18) * drawn
    return jnp.clip(drawn, min=-limit, max=limit).astype(kind)


def setup_inputs(seed: int = 0, part: int = 0) -> dict:
    seeds = jax.random.split(jax.random.key(seed), 6)
    part_splits = jax.random.split(jax.random.fold_in(seeds[5], part), 6)
    return {
        "volume": scatter_about(part_splits[0], (N_SPACE * 8, C, BLOCK_OUTPUT_X, BLOCK_OUTPUT_Y * BLOCK_OUTPUT_Z), 1.0, 6.0, ((0, 8),)),
        "kernel": scatter_about(seeds[1], (C, 27 * C), (27 * C) ** -0.5, 0.125),
        "beta": jnp.clip(jnp.exp(jax.random.uniform(seeds[2], (C,), jnp.float32, math.log(0.5), math.log(2.0))), 0.5, 2.0),
        "gamma": jnp.clip(jax.random.uniform(seeds[3], (C, C), jnp.float32, 0.0, 0.04), 0.0, 0.04),
        "cotangent": scatter_about(part_splits[4], (N_SPACE, C, BLOCK_OUTPUT_X, BLOCK_OUTPUT_Y * BLOCK_OUTPUT_Z), 1.0, 6.0, ((0, 8),)),
    }


def unblock_input(volume_array):
    groups = N_SPACE // 8
    shaped = volume_array.reshape(groups, 4, 2, 2, 2, 2, C, BLOCK_OUTPUT_X, BLOCK_OUTPUT_Y, BLOCK_OUTPUT_Z)
    return shaped.transpose(0, 7, 3, 1, 8, 4, 2, 9, 5, 6).reshape(groups * BLOCK_INPUT_X, 4 * BLOCK_INPUT_Y, 2 * BLOCK_INPUT_Z, C)

def regroup_input(grid):
    groups = N_SPACE // 8
    shaped = grid.reshape(groups, BLOCK_OUTPUT_X, 2, 4, BLOCK_OUTPUT_Y, 2, 2, BLOCK_OUTPUT_Z, 2, C)
    return shaped.transpose(0, 3, 6, 2, 5, 8, 9, 1, 4, 7).reshape(N_SPACE * 8, C, BLOCK_OUTPUT_X, BLOCK_OUTPUT_Y * BLOCK_OUTPUT_Z)

def unblock_output(array):
    groups = N_SPACE // 8
    shaped = array.reshape(groups, 4, 2, C, BLOCK_OUTPUT_X, BLOCK_OUTPUT_Y, BLOCK_OUTPUT_Z)
    return shaped.transpose(0, 4, 1, 5, 2, 6, 3).reshape(groups * BLOCK_OUTPUT_X, 4 * BLOCK_OUTPUT_Y, 2 * BLOCK_OUTPUT_Z, C)

def regroup_output(grid):
    groups = N_SPACE // 8
    shaped = grid.reshape(groups, BLOCK_OUTPUT_X, 4, BLOCK_OUTPUT_Y, 2, BLOCK_OUTPUT_Z, C)
    return shaped.transpose(0, 2, 4, 6, 1, 3, 5).reshape(N_SPACE, C, BLOCK_OUTPUT_X, BLOCK_OUTPUT_Y * BLOCK_OUTPUT_Z)

def convolve(grid, weights):
    return lax.conv_general_dilated(grid[None], weights, (2, 2, 2), ((1, 1), (1, 1), (1, 1)), dimension_numbers=('NDHWC', 'DHWIO', 'NDHWC'), precision=lax.Precision.HIGHEST)[0]

def reference(volume, kernel, beta, gamma, cotangent):
    highest = lax.Precision.HIGHEST
    grid = unblock_input(volume).astype(jnp.float32)
    weights = kernel.astype(jnp.float32).reshape(C, 3, 3, 3, C).transpose(1, 2, 3, 4, 0)
    convolved_output, pullback = jax.vjp(convolve, grid, weights)
    denom = beta + jnp.dot(convolved_output * convolved_output, gamma.T, precision=highest)
    reciprocal_norm = lax.rsqrt(denom)
    normalized = regroup_output((convolved_output * reciprocal_norm).astype(jnp.bfloat16))
    upstream = unblock_output(cotangent).astype(jnp.float32)
    weighted = -0.5 * upstream * convolved_output * reciprocal_norm * reciprocal_norm * reciprocal_norm
    grad_conv = (upstream * reciprocal_norm + 2.0 * convolved_output * jnp.dot(weighted, gamma, precision=highest)).astype(jnp.bfloat16)
    lattice_gradient, weight_grad = pullback(grad_conv.astype(jnp.float32))
    scale = 1.0 / math.sqrt(CELLS)
    volume_input_gradient = regroup_input(lattice_gradient.astype(jnp.bfloat16))
    kernel_grad = weight_grad.transpose(4, 0, 1, 2, 3).reshape(C, 27 * C) * scale
    flat_weighted = weighted.reshape(-1, C)
    flat_square = (convolved_output * convolved_output).reshape(-1, C)
    gamma_grad = jnp.dot(flat_weighted.T, flat_square, precision=highest) * scale
    beta_grad = lax.optimization_barrier(jnp.sum(flat_weighted, axis=0)) * scale
    return (normalized, volume_input_gradient, kernel_grad, gamma_grad, beta_grad)
```

```python
import functools
import math

import jax
import jax.numpy as jnp
from jax import lax
from jax.experimental import pallas as pl
from jax.experimental.pallas import tpu as pltpu
from jax.sharding import PartitionSpec as P

BF = jnp.bfloat16
F32 = jnp.float32
C = 96
NX = 8
LANES = 128
SZ = 16
ROWS = 9 * C
MESH = pl.DeviceIdType.MESH


def taps_of(parity):
    return ((1, 0),) if parity == 0 else ((2, 0), (0, 1))


def row_of(ty, tz):
    return (ty * 3 + tz) * C


def tile(x):
    return pl.ds(x * LANES, LANES)


def body(groups, scale, vol, ker, beta, gamma, cot, norm_o, dvol_o, kg_o, gg_o, bg_o,
         tmp, V, Yp, Zp, Yr, Zr, Cr, Kf, WB, Gs, up, S, GY, GZ, GYr, GZr, GCr,
         part, sendA, recvA, sendB, recvB, full, gacc, bacc,
         ysend, yrecv, zsend, zrecv, csend, crecv, xsend, xrecv,
         asend, arecv, bsend, brecv, gsend, grecv, dsend, drecv):
    idx = lax.axis_index("space")
    gx = idx // 8
    by = idx // 2 % 4
    bz = idx % 2
    base = gx * 8

    def dev(jy, jz):
        return {"space": base + jy * 2 + jz}

    barrier = pltpu.get_barrier_semaphore()
    for k in range(1, 8):
        peer = base + (idx - base + k) % 8
        pl.semaphore_signal(barrier, inc=1, device_id={"space": peer}, device_id_type=MESH)
    if groups > 1:
        @pl.when(gx > 0)
        def _():
            pl.semaphore_signal(barrier, inc=1, device_id={"space": idx - 8}, device_id_type=MESH)

        @pl.when(gx < groups - 1)
        def _():
            pl.semaphore_signal(barrier, inc=1, device_id={"space": idx + 8}, device_id_type=MESH)

    lane = lax.broadcasted_iota(jnp.int32, (C, LANES), 1)
    lz = lane % SZ
    ly = lane // SZ

    def roll(value, shift):
        shift = shift % LANES
        return value if shift == 0 else pltpu.roll(value, shift, 1)

    def remote(src, dst, ss, rs, target):
        return pltpu.make_async_remote_copy(
            src_ref=src, dst_ref=dst, send_sem=ss, recv_sem=rs,
            device_id=target, device_id_type=MESH)

    def spread_in(px, _):
        for py, pz in ((1, 1), (1, 0), (0, 1), (0, 0)):
            r = row_of(1 + py, 1 + pz)
            tmp[...] = vol[px * 4 + py * 2 + pz].astype(F32).reshape(C * NX, LANES)
            ya = jnp.zeros((C, LANES), F32)
            za = jnp.zeros((C, LANES), F32)
            for x in range(NX):
                t = tmp[pl.ds(x, C, stride=NX), :]
                V[px, r:r + C, tile(x + 1)] = t.astype(BF)
                if py:
                    ya = jnp.where(ly == x, roll(t, x * SZ - 112), ya)
                if pz:
                    za = jnp.where(lz == x, roll(t, x - 15), za)
            if py:
                Yp[px, pz] = ya.astype(BF)
            if pz:
                Zp[px, py] = za.astype(BF)
        return 0

    lax.fori_loop(0, 2, spread_in, 0)

    pl.semaphore_wait(barrier, 7)
    if groups > 1:
        @pl.when(gx > 0)
        def _():
            pl.semaphore_wait(barrier, 1)

        @pl.when(gx < groups - 1)
        def _():
            pl.semaphore_wait(barrier, 1)

    y_copy = remote(Yp, Yr, ysend, yrecv, dev((by + 1) % 4, bz))
    z_copy = remote(Zp, Zr, zsend, zrecv, dev(by, 1 - bz))
    c_copy = [remote(Yp.at[px, 1], Cr.at[px], csend.at[px], crecv.at[px], dev((by + 1) % 4, 1 - bz))
              for px in range(2)]

    @pl.when(by < 3)
    def _():
        y_copy.start()

        @pl.when(bz == 0)
        def _():
            for c in c_copy:
                c.start()

    @pl.when(bz == 0)
    def _():
        z_copy.start()

    for tx in range(3):
        Kf[tx] = ker[:, tx * ROWS:(tx + 1) * ROWS]
    WB[...] = jnp.zeros_like(WB)
    for tx in range(3):
        for py in range(2):
            for pz in range(2):
                q = (py * 2 + pz) * C
                for ty, sy in taps_of(py):
                    for tz, sz in taps_of(pz):
                        t = tx * 9 + ty * 3 + tz
                        w = ker[:, t * C:(t + 1) * C].astype(F32)
                        v = (sy * 2 + sz) * LANES
                        WB[tx, q:q + C, v:v + C] = w.T.astype(BF)
    for v in range(4):
        Gs[v * LANES + C:(v + 1) * LANES, :] = jnp.zeros((LANES - C, 9 * LANES), BF)
    if groups == 1:
        Gs[:, 8 * LANES:] = jnp.zeros((4 * LANES, LANES), BF)
        V[1, :, 0:LANES] = jnp.zeros((ROWS, LANES), BF)
    tmp[...] = cot[0].astype(F32).reshape(C * NX, LANES)
    for x in range(NX):
        up[:, tile(x)] = tmp[pl.ds(x, C, stride=NX), :]
    gam = gamma[...]
    gam_b = gam.astype(BF)
    gam_t = gam.T.astype(BF)
    eye = (lax.broadcasted_iota(jnp.int32, (C, C), 0) == lax.broadcasted_iota(jnp.int32, (C, C), 1))
    beta_col = jnp.sum(jnp.where(eye, beta[...], 0.0), axis=1, keepdims=True)

    @pl.when(by > 0)
    def _():
        y_copy.wait_recv()

        @pl.when(bz == 1)
        def _():
            for c in c_copy:
                c.wait_recv()

    @pl.when(by == 0)
    def _():
        Yr[...] = jnp.zeros_like(Yr)

    @pl.when((by == 0) | (bz == 0))
    def _():
        Cr[...] = jnp.zeros_like(Cr)

    @pl.when(bz == 1)
    def _():
        z_copy.wait_recv()

    @pl.when(bz == 0)
    def _():
        Zr[...] = jnp.zeros_like(Zr)

    def shifted(px, _):
        y0 = Yr[px, 0].astype(F32)
        y1 = Yr[px, 1].astype(F32)
        z0 = Zr[px, 0].astype(F32)
        z1 = Zr[px, 1].astype(F32)
        yz = jnp.where(lz == 0, roll(Cr[px].astype(F32), -15), roll(y1, 1))
        for x in range(NX):
            def get(ty, tz):
                r = row_of(ty, tz)
                return V[px, r:r + C, tile(x + 1)].astype(F32)

            def put(ty, tz, value):
                r = row_of(ty, tz)
                V[px, r:r + C, tile(x + 1)] = value.astype(BF)

            put(1, 0, jnp.where(lz == 0, roll(z0, -x), roll(get(1, 2), 1)))
            put(0, 1, jnp.where(ly == 0, roll(y0, -SZ * x), roll(get(2, 1), SZ)))
            d = get(2, 2)
            t = jnp.where(lz == 0, roll(z1, -x), roll(d, 1))
            put(2, 0, t)
            put(0, 2, jnp.where(ly == 0, roll(y1, -SZ * x), roll(d, SZ)))
            put(0, 0, jnp.where(ly == 0, roll(yz, -SZ * x), roll(t, SZ)))
        return 0

    lax.fori_loop(0, 2, shifted, 0)

    if groups > 1:
        x_copy = remote(V.at[1, :, pl.ds(8 * LANES, LANES)], V.at[1, :, pl.ds(0, LANES)],
                        xsend.at[0], xrecv.at[0], {"space": (idx + 8) % (groups * 8)})

        @pl.when(gx < groups - 1)
        def _():
            x_copy.start()

        @pl.when(gx > 0)
        def _():
            x_copy.wait_recv()

        @pl.when(gx == 0)
        def _():
            V[1, :, 0:LANES] = jnp.zeros((ROWS, LANES), BF)

    gacc[...] = jnp.zeros_like(gacc)
    bacc[...] = jnp.zeros_like(bacc)

    def forward(i, _):
        lo = pl.multiple_of(i * 256, 256)
        hi = pl.multiple_of(i * 256 + LANES, LANES)
        conv = jnp.dot(Kf[1], V[0, :, pl.ds(hi, 256)], preferred_element_type=F32)
        conv += jnp.dot(Kf[0], V[1, :, pl.ds(lo, 256)], preferred_element_type=F32)
        conv += jnp.dot(Kf[2], V[1, :, pl.ds(hi, 256)], preferred_element_type=F32)
        sq = conv * conv
        sq_b = sq.astype(BF)
        r = lax.rsqrt(beta_col + jnp.dot(gam_b, sq_b, preferred_element_type=F32))
        u = up[:, pl.ds(lo, 256)]
        normalized = conv * r
        weighted = -0.5 * u * conv * r * r * r
        w_b = weighted.astype(BF)
        coupled = jnp.dot(gam_t, w_b, preferred_element_type=F32)
        g = u * r + 2.0 * conv * coupled
        Gs[0:C, pl.ds(lo, 256)] = g.astype(BF)
        gacc[...] += lax.dot_general(w_b, sq_b, (((1,), (1,)), ((), ())), preferred_element_type=F32)
        bacc[...] += weighted[:, :LANES] + weighted[:, LANES:]
        for xx in range(2):
            tmp[pl.ds(i * 2 + xx, C, stride=NX), :] = normalized[:, xx * LANES:(xx + 1) * LANES]
        return 0

    lax.fori_loop(0, 4, forward, 0)
    norm_o[0] = tmp[...].reshape(C, NX, LANES).astype(BF)

    ya = jnp.zeros((C, LANES), F32)
    za = jnp.zeros((C, LANES), F32)
    for x in range(NX):
        t = Gs[0:C, tile(x)].astype(F32)
        ya = jnp.where(ly == x, roll(t, x * SZ), ya)
        za = jnp.where(lz == x, roll(t, x), za)
    GY[...] = ya.astype(BF)
    GZ[...] = za.astype(BF)
    gy_copy = remote(GY, GYr, gsend.at[0], grecv.at[0], dev((by + 3) % 4, bz))
    gz_copy = remote(GZ, GZr, gsend.at[1], grecv.at[1], dev(by, 1 - bz))
    gc_copy = remote(GY, GCr, gsend.at[2], grecv.at[2], dev((by + 3) % 4, 1 - bz))

    @pl.when(by > 0)
    def _():
        gy_copy.start()

        @pl.when(bz == 1)
        def _():
            gc_copy.start()

    @pl.when(bz == 1)
    def _():
        gz_copy.start()

    nt = (((1,), (1,)), ((), ()))
    for tx in range(3):
        first = 0 if tx == 0 else LANES
        plane = 0 if tx == 1 else 1
        for s in range(4):
            n = min(256, ROWS - s * 256)
            k = lax.dot_general(Gs[0:C, 0:8 * LANES],
                                V[plane, s * 256:s * 256 + n, first:first + 8 * LANES],
                                nt, preferred_element_type=F32) * scale
            if n == 256:
                part[tx * 7 + s * 2] = k[:, :LANES]
                part[tx * 7 + s * 2 + 1] = k[:, LANES:]
            else:
                part[tx * 7 + s * 2] = jnp.concatenate([k, jnp.zeros((C, LANES - C), F32)], axis=1)
    bsum = jnp.sum(bacc[...], axis=1, keepdims=True) * scale
    part[21] = jnp.concatenate(
        [gacc[...] * scale, jnp.broadcast_to(bsum, (C, LANES - C))], axis=1)
    part[22] = jnp.zeros((C, LANES), F32)
    part[23] = jnp.zeros((C, LANES), F32)

    def to_a(i, _):
        sendA[i] = part[(1 - bz) * 12 + i].astype(BF)
        return 0

    lax.fori_loop(0, 12, to_a, 0)
    a_copy = remote(sendA, recvA, asend, arecv, dev(by, 1 - bz))
    a_copy.start()

    @pl.when(by < 3)
    def _():
        gy_copy.wait_recv()

        @pl.when(bz == 0)
        def _():
            gc_copy.wait_recv()

    @pl.when(bz == 0)
    def _():
        gz_copy.wait_recv()

    @pl.when(by == 3)
    def _():
        GYr[...] = jnp.zeros_like(GYr)

    @pl.when((by == 3) | (bz == 1))
    def _():
        GCr[...] = jnp.zeros_like(GCr)

    @pl.when(bz == 1)
    def _():
        GZr[...] = jnp.zeros_like(GZr)

    y = GYr[...].astype(F32)
    z = GZr[...].astype(F32)
    yz = jnp.where(lz == SZ - 1, roll(GCr[...].astype(F32), 15), roll(y, -1))
    for x in range(NX):
        g = Gs[0:C, tile(x)].astype(F32)
        t = jnp.where(lz == SZ - 1, roll(z, 15 - x), roll(g, -1))
        Gs[LANES:LANES + C, tile(x)] = t.astype(BF)
        Gs[2 * LANES:2 * LANES + C, tile(x)] = jnp.where(
            ly == 7, roll(y, 112 - SZ * x), roll(g, -SZ)).astype(BF)
        Gs[3 * LANES:3 * LANES + C, tile(x)] = jnp.where(
            ly == 7, roll(yz, 112 - SZ * x), roll(t, -SZ)).astype(BF)

    if groups > 1:
        h_copy = remote(Gs.at[:, pl.ds(0, LANES)], Gs.at[:, pl.ds(8 * LANES, LANES)],
                        xsend.at[1], xrecv.at[1], {"space": (idx + (groups - 1) * 8) % (groups * 8)})

        @pl.when(gx > 0)
        def _():
            h_copy.start()

        @pl.when(gx < groups - 1)
        def _():
            h_copy.wait_recv()

        @pl.when(gx == groups - 1)
        def _():
            Gs[:, 8 * LANES:] = jnp.zeros((4 * LANES, LANES), BF)

    a_copy.wait()

    def add_a(i, _):
        j = bz * 12 + i
        total = part[j] + recvA[i].astype(F32)
        part[j] = total
        sendB[i // 3, i % 3] = total.astype(BF)
        return 0

    lax.fori_loop(0, 12, add_a, 0)
    b_copy = []
    for k in range(1, 4):
        to = (by + k) % 4
        b_copy.append(remote(sendB.at[to], recvB.at[k], bsend.at[k], brecv.at[k], dev(to, bz)))
        b_copy[-1].start()

    def back(px):
        def step(i, _):
            lo = pl.multiple_of(i * 256, 256)
            hi = pl.multiple_of(i * 256 + LANES, LANES)
            if px == 0:
                res = jnp.dot(WB[1], Gs[:, pl.ds(lo, 256)], preferred_element_type=F32)
            else:
                res = jnp.dot(WB[2], Gs[:, pl.ds(lo, 256)], preferred_element_type=F32)
                res += jnp.dot(WB[0], Gs[:, pl.ds(hi, 256)], preferred_element_type=F32)
            for q in range(4):
                for xx in range(2):
                    S[pl.ds(q * C * NX + i * 2 + xx, C, stride=NX), :] = (
                        res[q * C:(q + 1) * C, xx * LANES:(xx + 1) * LANES])
            return 0

        lax.fori_loop(0, 4, step, 0)
        for q in range(4):
            dvol_o[px * 4 + q] = S[q * C * NX:(q + 1) * C * NX].reshape(C, NX, LANES).astype(BF)

    back(0)

    for c in b_copy:
        c.wait()
    for i in range(3):
        total = part[bz * 12 + by * 3 + i]
        for k in range(1, 4):
            total += recvB[k, i].astype(F32)
        full[bz, by, i] = total.astype(BF)
    d_copy = []
    for k in range(1, 4):
        to = (by + k) % 4
        d_copy.append(remote(full.at[bz, by], full.at[bz, by], dsend.at[k], drecv.at[k], dev(to, bz)))
        d_copy[-1].start()

    back(1)

    for k in range(1, 4):
        source = (by + 4 - k) % 4
        remote(full.at[bz, source], full.at[bz, source], dsend.at[k], drecv.at[k],
               dev((by + k) % 4, bz)).wait()
    e_copy = remote(full.at[bz], full.at[bz], dsend.at[0], drecv.at[0], dev(by, 1 - bz))
    e_copy.start()
    e_copy.wait_send()
    remote(full.at[1 - bz], full.at[1 - bz], dsend.at[0], drecv.at[0], dev(by, 1 - bz)).wait_recv()

    for tx in range(3):
        for s in range(7):
            j = tx * 7 + s
            n = min(LANES, ROWS - s * LANES)
            at = tx * ROWS + s * LANES
            kg_o[:, at:at + n] = full[j // 12, j % 12 // 3, j % 3][:, :n].astype(F32)
    last = full[1, 3, 0].astype(F32)
    gg_o[...] = last[:, :C]
    bg_o[...] = jnp.sum(jnp.where(eye, last[:, C:C + 1], 0.0), axis=0, keepdims=True)

    @pl.when(by < 3)
    def _():
        y_copy.wait_send()

        @pl.when(bz == 0)
        def _():
            for c in c_copy:
                c.wait_send()

    @pl.when(bz == 0)
    def _():
        z_copy.wait_send()

    @pl.when(by > 0)
    def _():
        gy_copy.wait_send()

        @pl.when(bz == 1)
        def _():
            gc_copy.wait_send()

    @pl.when(bz == 1)
    def _():
        gz_copy.wait_send()

    if groups > 1:
        @pl.when(gx < groups - 1)
        def _():
            x_copy.wait_send()

        @pl.when(gx > 0)
        def _():
            h_copy.wait_send()


def shards(volume, kernel, beta, gamma, cotangent):
    devices = lax.axis_size("space")
    groups = devices // 8
    scale = 1.0 / math.sqrt(NX * LANES * devices)
    vm = lambda *shape, dtype=BF: pltpu.VMEM(shape, dtype)
    dma = lambda *shape: pltpu.SemaphoreType.DMA(shape) if shape else pltpu.SemaphoreType.DMA
    spec = pl.BlockSpec(memory_space=pltpu.VMEM)
    out = pl.pallas_call(
        functools.partial(body, groups, scale),
        out_shape=(
            jax.ShapeDtypeStruct((1, C, NX, LANES), BF),
            jax.ShapeDtypeStruct((8, C, NX, LANES), BF),
            jax.ShapeDtypeStruct((C, 27 * C), F32),
            jax.ShapeDtypeStruct((C, C), F32),
            jax.ShapeDtypeStruct((1, C), F32),
        ),
        in_specs=[spec] * 5,
        out_specs=(spec,) * 5,
        scratch_shapes=[
            vm(C * NX, LANES, dtype=F32), vm(2, ROWS, 9 * LANES),
            vm(2, 2, C, LANES), vm(2, 2, C, LANES), vm(2, 2, C, LANES), vm(2, 2, C, LANES), vm(2, C, LANES),
            vm(3, C, ROWS), vm(3, 4 * C, 4 * LANES), vm(4 * LANES, 9 * LANES),
            vm(C, NX * LANES, dtype=F32), vm(4 * C * NX, LANES, dtype=F32),
            vm(C, LANES), vm(C, LANES), vm(C, LANES), vm(C, LANES), vm(C, LANES),
            vm(24, C, LANES, dtype=F32), vm(12, C, LANES), vm(12, C, LANES),
            vm(4, 3, C, LANES), vm(4, 3, C, LANES), vm(2, 4, 3, C, LANES),
            vm(C, C, dtype=F32), vm(C, LANES, dtype=F32),
            dma(), dma(), dma(), dma(), dma(2), dma(2), dma(2), dma(2),
            dma(), dma(), dma(4), dma(4), dma(3), dma(3), dma(4), dma(4),
        ],
        compiler_params=pltpu.CompilerParams(
            collective_id=0, has_side_effects=True, vmem_limit_bytes=48 * 1024 * 1024),
    )(volume, kernel, beta.reshape(1, C), gamma, cotangent)
    normalized, dvol, kg, gg, bg = out
    if groups > 1:
        kg, gg, bg = jax.tree.map(lambda a: a * 0.125, lax.psum((kg, gg, bg), "space"))
    return normalized, dvol, kg, gg, bg.reshape(C)


def solution(mesh):
    blocks = P(("dp", "space"), None, None, None)
    return jax.shard_map(
        shards,
        mesh=mesh,
        in_specs=(blocks, P(), P(), P(), blocks),
        out_specs=(blocks, blocks, P("dp", None), P("dp", None), P("dp")),
        check_vma=False,
    )
```

```python
import functools
import math

import jax
import jax.numpy as jnp
from jax import lax
from jax.experimental import pallas as pl
from jax.experimental.pallas import tpu as pltpu
from jax.sharding import PartitionSpec as P

BF = jnp.bfloat16
F32 = jnp.float32
C = 96
NX = 8
LANES = 128
SZ = 16
ROWS = 9 * C
DEPTH = 1024
MESH = pl.DeviceIdType.MESH


def taps_of(parity):
    return ((1, 0),) if parity == 0 else ((2, 0), (0, 1))


def row_of(ty, tz):
    return (ty * 3 + tz) * C


def tile(x):
    return pl.ds(x * LANES, LANES)


def body(groups, scale, vol_h, ker_h, beta_h, gamma_h, cot_h, norm_h, dvol_h, full_h,
         norm_o, dvol_o, full, out_sem, vol, ker, beta, gamma, cot, tmp, V, Yp, Zp, Yr, Zr, Cr, Kf, WB, Gs, up, S, GY, GZ, GYr, GZr, GCr,
         part, gslab, sendA, recvA, sendB, recvB, gacc, bacc, in_sem,
         ysend, yrecv, zsend, zrecv, csend, crecv, xsend, xrecv,
         asend, arecv, bsend, brecv, gsend, grecv, dsend, drecv, esend, erecv):
    idx = lax.axis_index("space")
    gx = idx // 8
    by = idx // 2 % 4
    bz = idx % 2
    base = gx * 8

    def dev(jy, jz):
        return {"space": base + jy * 2 + jz}

    loads = [pltpu.make_async_copy(vol_h.at[pl.ds(4 * i, 4)], vol.at[pl.ds(4 * i, 4)], in_sem.at[i])
             for i in range(2)]
    loads += [pltpu.make_async_copy(src, dst, in_sem.at[2 + i]) for i, (src, dst) in enumerate(
        ((ker_h, ker), (cot_h, cot), (gamma_h, gamma), (beta_h, beta)))]
    for load in loads:
        load.start()

    barrier = pltpu.get_barrier_semaphore()
    for k in range(1, 8):
        peer = base + (idx - base + k) % 8
        pl.semaphore_signal(barrier, inc=1, device_id={"space": peer}, device_id_type=MESH)
    if groups > 1:
        @pl.when(gx > 0)
        def _():
            pl.semaphore_signal(barrier, inc=1, device_id={"space": idx - 8}, device_id_type=MESH)

        @pl.when(gx < groups - 1)
        def _():
            pl.semaphore_signal(barrier, inc=1, device_id={"space": idx + 8}, device_id_type=MESH)

    lane = lax.broadcasted_iota(jnp.int32, (C, LANES), 1)
    lz = lane % SZ
    ly = lane // SZ

    def roll(value, shift):
        shift = shift % LANES
        return value if shift == 0 else pltpu.roll(value, shift, 1)

    def remote(src, dst, ss, rs, target):
        return pltpu.make_async_remote_copy(
            src_ref=src, dst_ref=dst, send_sem=ss, recv_sem=rs,
            device_id=target, device_id_type=MESH)

    def spread_in(px, _):
        for py, pz in ((1, 1), (1, 0), (0, 1), (0, 0)):
            r = row_of(1 + py, 1 + pz)
            tmp[...] = vol[px * 4 + py * 2 + pz].astype(F32).reshape(C * NX, LANES)
            ya = jnp.zeros((C, LANES), F32)
            za = jnp.zeros((C, LANES), F32)
            for x in range(NX):
                t = tmp[pl.ds(x, C, stride=NX), :]
                V[px, r:r + C, tile(x + 1)] = t.astype(BF)
                if py:
                    ya = jnp.where(ly == x, roll(t, x * SZ - 112), ya)
                if pz:
                    za = jnp.where(lz == x, roll(t, x - 15), za)
            if py:
                Yp[px, pz] = ya.astype(BF)
            if pz:
                Zp[px, py] = za.astype(BF)
        return 0

    loads[0].wait()
    loads[1].wait()
    lax.fori_loop(0, 2, spread_in, 0)

    pl.semaphore_wait(barrier, 7)
    if groups > 1:
        @pl.when(gx > 0)
        def _():
            pl.semaphore_wait(barrier, 1)

        @pl.when(gx < groups - 1)
        def _():
            pl.semaphore_wait(barrier, 1)

    y_copy = remote(Yp, Yr, ysend, yrecv, dev((by + 1) % 4, bz))
    z_copy = remote(Zp, Zr, zsend, zrecv, dev(by, 1 - bz))
    c_copy = [remote(Yp.at[px, 1], Cr.at[px], csend.at[px], crecv.at[px], dev((by + 1) % 4, 1 - bz))
              for px in range(2)]

    @pl.when(by < 3)
    def _():
        y_copy.start()

        @pl.when(bz == 0)
        def _():
            for c in c_copy:
                c.start()

    @pl.when(bz == 0)
    def _():
        z_copy.start()

    for load in loads[2:]:
        load.wait()
    for tx in range(3):
        Kf[tx] = ker[:, tx * ROWS:(tx + 1) * ROWS]
    WB[...] = jnp.zeros_like(WB)
    for tx in range(3):
        for py in range(2):
            for pz in range(2):
                q = (py * 2 + pz) * C
                for ty, sy in taps_of(py):
                    for tz, sz in taps_of(pz):
                        t = tx * 9 + ty * 3 + tz
                        w = ker[:, t * C:(t + 1) * C].astype(F32)
                        v = (sy * 2 + sz) * LANES
                        WB[tx, q:q + C, v:v + C] = w.T.astype(BF)
    for v in range(4):
        Gs[v * LANES + C:(v + 1) * LANES, :] = jnp.zeros((LANES - C, 9 * LANES), BF)
    if groups == 1:
        Gs[:, 8 * LANES:] = jnp.zeros((4 * LANES, LANES), BF)
        V[1, :, 0:LANES] = jnp.zeros((DEPTH, LANES), BF)
    V[:, ROWS:, :] = jnp.zeros((2, DEPTH - ROWS, 9 * LANES), BF)
    tmp[...] = cot[0].astype(F32).reshape(C * NX, LANES)
    for x in range(NX):
        up[:, tile(x)] = tmp[pl.ds(x, C, stride=NX), :]
    gam = gamma[...]
    gam_b = gam.astype(BF)
    gam_t = gam.T.astype(BF)
    eye = (lax.broadcasted_iota(jnp.int32, (C, C), 0) == lax.broadcasted_iota(jnp.int32, (C, C), 1))
    beta_col = jnp.sum(jnp.where(eye, beta[...], 0.0), axis=1, keepdims=True)

    @pl.when(by > 0)
    def _():
        y_copy.wait_recv()

        @pl.when(bz == 1)
        def _():
            for c in c_copy:
                c.wait_recv()

    @pl.when(by == 0)
    def _():
        Yr[...] = jnp.zeros_like(Yr)

    @pl.when((by == 0) | (bz == 0))
    def _():
        Cr[...] = jnp.zeros_like(Cr)

    @pl.when(bz == 1)
    def _():
        z_copy.wait_recv()

    @pl.when(bz == 0)
    def _():
        Zr[...] = jnp.zeros_like(Zr)

    def shifted(px, _):
        y0 = Yr[px, 0].astype(F32)
        y1 = Yr[px, 1].astype(F32)
        z0 = Zr[px, 0].astype(F32)
        z1 = Zr[px, 1].astype(F32)
        yz = jnp.where(lz == 0, roll(Cr[px].astype(F32), -15), roll(y1, 1))
        for x in range(NX):
            def get(ty, tz):
                r = row_of(ty, tz)
                return V[px, r:r + C, tile(x + 1)].astype(F32)

            def put(ty, tz, value):
                r = row_of(ty, tz)
                V[px, r:r + C, tile(x + 1)] = value.astype(BF)

            put(1, 0, jnp.where(lz == 0, roll(z0, -x), roll(get(1, 2), 1)))
            put(0, 1, jnp.where(ly == 0, roll(y0, -SZ * x), roll(get(2, 1), SZ)))
            d = get(2, 2)
            t = jnp.where(lz == 0, roll(z1, -x), roll(d, 1))
            put(2, 0, t)
            put(0, 2, jnp.where(ly == 0, roll(y1, -SZ * x), roll(d, SZ)))
            put(0, 0, jnp.where(ly == 0, roll(yz, -SZ * x), roll(t, SZ)))
        return 0

    lax.fori_loop(0, 2, shifted, 0)

    if groups > 1:
        x_copy = remote(V.at[1, :, pl.ds(8 * LANES, LANES)], V.at[1, :, pl.ds(0, LANES)],
                        xsend.at[0], xrecv.at[0], {"space": (idx + 8) % (groups * 8)})

        @pl.when(gx < groups - 1)
        def _():
            x_copy.start()

        @pl.when(gx > 0)
        def _():
            x_copy.wait_recv()

        @pl.when(gx == 0)
        def _():
            V[1, :, 0:LANES] = jnp.zeros((DEPTH, LANES), BF)

    gacc[...] = jnp.zeros_like(gacc)
    bacc[...] = jnp.zeros_like(bacc)

    def forward(i, _):
        lo = pl.multiple_of(i * 256, 256)
        hi = pl.multiple_of(i * 256 + LANES, LANES)
        conv = jnp.dot(Kf[1], V[0, 0:ROWS, pl.ds(hi, 256)], preferred_element_type=F32)
        conv += jnp.dot(Kf[0], V[1, 0:ROWS, pl.ds(lo, 256)], preferred_element_type=F32)
        conv += jnp.dot(Kf[2], V[1, 0:ROWS, pl.ds(hi, 256)], preferred_element_type=F32)
        sq = conv * conv
        sq_b = sq.astype(BF)
        r = lax.rsqrt(beta_col + jnp.dot(gam_b, sq_b, preferred_element_type=F32))
        u = up[:, pl.ds(lo, 256)]
        normalized = conv * r
        weighted = -0.5 * u * conv * r * r * r
        w_b = weighted.astype(BF)
        coupled = jnp.dot(gam_t, w_b, preferred_element_type=F32)
        g = u * r + 2.0 * conv * coupled
        Gs[0:C, pl.ds(lo, 256)] = g.astype(BF)
        gacc[...] += lax.dot_general(w_b, sq_b, (((1,), (1,)), ((), ())), preferred_element_type=F32)
        bacc[...] += weighted[:, :LANES] + weighted[:, LANES:]
        for xx in range(2):
            tmp[pl.ds(i * 2 + xx, C, stride=NX), :] = normalized[:, xx * LANES:(xx + 1) * LANES]
        return 0

    lax.fori_loop(0, 4, forward, 0)
    norm_o[0] = tmp[...].reshape(C, NX, LANES).astype(BF)
    stores = [pltpu.make_async_copy(norm_o, norm_h, out_sem.at[0])]
    stores[0].start()

    ya = jnp.zeros((C, LANES), F32)
    za = jnp.zeros((C, LANES), F32)
    for x in range(NX):
        t = Gs[0:C, tile(x)].astype(F32)
        ya = jnp.where(ly == x, roll(t, x * SZ), ya)
        za = jnp.where(lz == x, roll(t, x), za)
    GY[...] = ya.astype(BF)
    GZ[...] = za.astype(BF)
    gy_copy = remote(GY, GYr, gsend.at[0], grecv.at[0], dev((by + 3) % 4, bz))
    gz_copy = remote(GZ, GZr, gsend.at[1], grecv.at[1], dev(by, 1 - bz))
    gc_copy = remote(GY, GCr, gsend.at[2], grecv.at[2], dev((by + 3) % 4, 1 - bz))

    @pl.when(by > 0)
    def _():
        gy_copy.start()

        @pl.when(bz == 1)
        def _():
            gc_copy.start()

    @pl.when(bz == 1)
    def _():
        gz_copy.start()

    nt = (((1,), (1,)), ((), ()))
    bsum = jnp.sum(bacc[...], axis=1, keepdims=True) * scale
    gslab[...] = jnp.concatenate(
        [gacc[...] * scale, jnp.broadcast_to(bsum, (C, LANES - C))], axis=1)

    def slabs(pair):
        tx = pair // 4
        row = pl.multiple_of(pair % 4 * 256, 256)
        first = pl.multiple_of((tx + 1) // 2 * LANES, LANES)
        k = lax.dot_general(Gs[0:C, 0:8 * LANES],
                            V[(tx + 1) % 2, pl.ds(row, 256), pl.ds(first, 8 * LANES)],
                            nt, preferred_element_type=F32) * scale
        return k[:, :LANES], k[:, LANES:] + jnp.where(pair == 11, gslab[...], 0.0)

    def a_copy(i):
        return remote(sendA.at[pl.ds(2 * i, 2)], recvA.at[pl.ds(2 * i, 2)], asend.at[i], arecv.at[i],
                      dev(by, 1 - bz))

    def theirs(i, _):
        low, high = slabs((1 - bz) * 6 + i)
        sendA[2 * i] = low.astype(BF)
        sendA[2 * i + 1] = high.astype(BF)
        a_copy(i).start()
        return 0

    lax.fori_loop(0, 6, theirs, 0)

    def ours(i, _):
        low, high = slabs(bz * 6 + i)
        part[2 * i] = low
        part[2 * i + 1] = high
        return 0

    lax.fori_loop(0, 6, ours, 0)

    def wait_a(i, _):
        a_copy(i).wait()
        return 0

    lax.fori_loop(0, 6, wait_a, 0)
    b_copy = []
    for k in (2, 1, 3):
        to = (by + k) % 4
        for i in range(3):
            j = to * 3 + i
            sendB[k, i] = (part[j] + recvA[j].astype(F32)).astype(BF)
        b_copy.append(remote(sendB.at[k], recvB.at[k], bsend.at[k], brecv.at[k], dev(to, bz)))
        b_copy[-1].start()

    @pl.when(by < 3)
    def _():
        gy_copy.wait_recv()

        @pl.when(bz == 0)
        def _():
            gc_copy.wait_recv()

    @pl.when(bz == 0)
    def _():
        gz_copy.wait_recv()

    @pl.when(by == 3)
    def _():
        GYr[...] = jnp.zeros_like(GYr)

    @pl.when((by == 3) | (bz == 1))
    def _():
        GCr[...] = jnp.zeros_like(GCr)

    @pl.when(bz == 1)
    def _():
        GZr[...] = jnp.zeros_like(GZr)

    y = GYr[...].astype(F32)
    z = GZr[...].astype(F32)
    yz = jnp.where(lz == SZ - 1, roll(GCr[...].astype(F32), 15), roll(y, -1))
    for x in range(NX):
        g = Gs[0:C, tile(x)].astype(F32)
        t = jnp.where(lz == SZ - 1, roll(z, 15 - x), roll(g, -1))
        Gs[LANES:LANES + C, tile(x)] = t.astype(BF)
        Gs[2 * LANES:2 * LANES + C, tile(x)] = jnp.where(
            ly == 7, roll(y, 112 - SZ * x), roll(g, -SZ)).astype(BF)
        Gs[3 * LANES:3 * LANES + C, tile(x)] = jnp.where(
            ly == 7, roll(yz, 112 - SZ * x), roll(t, -SZ)).astype(BF)

    if groups > 1:
        h_copy = remote(Gs.at[:, pl.ds(0, LANES)], Gs.at[:, pl.ds(8 * LANES, LANES)],
                        xsend.at[1], xrecv.at[1], {"space": (idx + (groups - 1) * 8) % (groups * 8)})

        @pl.when(gx > 0)
        def _():
            h_copy.start()

        @pl.when(gx < groups - 1)
        def _():
            h_copy.wait_recv()

        @pl.when(gx == groups - 1)
        def _():
            Gs[:, 8 * LANES:] = jnp.zeros((4 * LANES, LANES), BF)

    def back(px):
        def step(i, _):
            lo = pl.multiple_of(i * 256, 256)
            hi = pl.multiple_of(i * 256 + LANES, LANES)
            if px == 0:
                res = jnp.dot(WB[1], Gs[:, pl.ds(lo, 256)], preferred_element_type=F32)
            else:
                res = jnp.dot(WB[2], Gs[:, pl.ds(lo, 256)], preferred_element_type=F32)
                res += jnp.dot(WB[0], Gs[:, pl.ds(hi, 256)], preferred_element_type=F32)
            for q in range(4):
                for xx in range(2):
                    S[pl.ds(q * C * NX + i * 2 + xx, C, stride=NX), :] = (
                        res[q * C:(q + 1) * C, xx * LANES:(xx + 1) * LANES])
            return 0

        lax.fori_loop(0, 4, step, 0)
        for q in range(4):
            dvol_o[px * 4 + q] = S[q * C * NX:(q + 1) * C * NX].reshape(C, NX, LANES).astype(BF)
        stores.append(pltpu.make_async_copy(
            dvol_o.at[pl.ds(4 * px, 4)], dvol_h.at[pl.ds(4 * px, 4)], out_sem.at[1 + px]))
        stores[-1].start()

    back(0)

    for c in b_copy:
        c.wait()
    for i in range(3):
        total = part[by * 3 + i] + recvA[by * 3 + i].astype(F32)
        for k in range(1, 4):
            total += recvB[k, i].astype(F32)
        full[bz, by, i] = total.astype(BF)
    d_copy = []
    for k in (2, 1, 3):
        to = (by + k) % 4
        d_copy.append(remote(full.at[bz, by], full.at[bz, by], dsend.at[k], drecv.at[k], dev(to, bz)))
        d_copy[-1].start()

    def e_copy(half, k):
        source = (by + 4 - k) % 4
        return remote(full.at[half, source], full.at[half, source], esend.at[k], erecv.at[k],
                      dev(by, 1 - bz))

    e_copy(bz, 0).start()

    back(1)

    for k in (1, 3, 2):
        source = (by + 4 - k) % 4
        remote(full.at[bz, source], full.at[bz, source], dsend.at[k], drecv.at[k],
               dev((by + k) % 4, bz)).wait_recv()
        e_copy(bz, k).start()
    for k in range(4):
        e_copy(1 - bz, k).wait_recv()
        e_copy(bz, k).wait_send()
    for d in d_copy:
        d.wait_send()

    stores.append(pltpu.make_async_copy(full, full_h, out_sem.at[3]))
    stores[-1].start()
    for store in stores:
        store.wait()

    @pl.when(by < 3)
    def _():
        y_copy.wait_send()

        @pl.when(bz == 0)
        def _():
            for c in c_copy:
                c.wait_send()

    @pl.when(bz == 0)
    def _():
        z_copy.wait_send()

    @pl.when(by > 0)
    def _():
        gy_copy.wait_send()

        @pl.when(bz == 1)
        def _():
            gc_copy.wait_send()

    @pl.when(bz == 1)
    def _():
        gz_copy.wait_send()

    if groups > 1:
        @pl.when(gx < groups - 1)
        def _():
            x_copy.wait_send()

        @pl.when(gx > 0)
        def _():
            h_copy.wait_send()


def finish(norm, dvol, full_h, norm_o, dvol_o, kg_o, gg_o, bg_o, full, kg, gg, bg, norm_v, dvol_v, sem):
    load = pltpu.make_async_copy(full_h, full, sem.at[5])
    load.start()
    fetch = [pltpu.make_async_copy(dvol.at[pl.ds(2 * i, 2)], dvol_v.at[pl.ds(2 * i, 2)], sem.at[6 + i])
             for i in range(4)]
    fetch.append(pltpu.make_async_copy(norm, norm_v, sem.at[10]))
    for f in fetch:
        f.start()
    copies = [pltpu.make_async_copy(dvol_v, dvol_o, sem.at[0]), pltpu.make_async_copy(norm_v, norm_o, sem.at[1])]
    for f in fetch:
        f.wait()
    for c in copies:
        c.start()
    load.wait()
    for tx in range(3):
        for s in range(7):
            j = tx * 8 + s
            n = min(LANES, ROWS - s * LANES)
            at = tx * ROWS + s * LANES
            kg[:, at:at + n] = full[j // 12, j % 12 // 3, j % 3][:, :n].astype(F32)
    copies.append(pltpu.make_async_copy(kg, kg_o, sem.at[2]))
    copies[-1].start()
    last = full[1, 3, 2].astype(F32)
    eye = (lax.broadcasted_iota(jnp.int32, (C, C), 0) == lax.broadcasted_iota(jnp.int32, (C, C), 1))
    gg[...] = last[:, :C]
    bg[...] = jnp.sum(jnp.where(eye, last[:, C:C + 1], 0.0), axis=0, keepdims=True)
    copies.append(pltpu.make_async_copy(gg, gg_o, sem.at[3]))
    copies.append(pltpu.make_async_copy(bg, bg_o, sem.at[4]))
    copies[3].start()
    copies[4].start()
    for c in copies:
        c.wait()


def shards(volume, kernel, beta, gamma, cotangent):
    devices = lax.axis_size("space")
    groups = devices // 8
    scale = 1.0 / math.sqrt(NX * LANES * devices)
    vm = lambda *shape, dtype=BF: pltpu.VMEM(shape, dtype)
    dma = lambda *shape: pltpu.SemaphoreType.DMA(shape) if shape else pltpu.SemaphoreType.DMA
    hbm = pl.BlockSpec(memory_space=pltpu.HBM)
    norm, dvol, full = pl.pallas_call(
        functools.partial(body, groups, scale),
        out_shape=(
            jax.ShapeDtypeStruct((1, C, NX, LANES), BF),
            jax.ShapeDtypeStruct((8, C, NX, LANES), BF),
            jax.ShapeDtypeStruct((2, 4, 3, C, LANES), BF),
        ),
        in_specs=[hbm] * 5,
        out_specs=(hbm,) * 3,
        scratch_shapes=[
            vm(1, C, NX, LANES), vm(8, C, NX, LANES), vm(2, 4, 3, C, LANES), dma(4),
            vm(8, C, NX, LANES), vm(C, 27 * C), vm(1, C, dtype=F32), vm(C, C, dtype=F32), vm(1, C, NX, LANES),
            vm(C * NX, LANES, dtype=F32), vm(2, DEPTH, 9 * LANES),
            vm(2, 2, C, LANES), vm(2, 2, C, LANES), vm(2, 2, C, LANES), vm(2, 2, C, LANES), vm(2, C, LANES),
            vm(3, C, ROWS), vm(3, 4 * C, 4 * LANES), vm(4 * LANES, 9 * LANES),
            vm(C, NX * LANES, dtype=F32), vm(4 * C * NX, LANES, dtype=F32),
            vm(C, LANES), vm(C, LANES), vm(C, LANES), vm(C, LANES), vm(C, LANES),
            vm(12, C, LANES, dtype=F32), vm(C, LANES, dtype=F32), vm(12, C, LANES), vm(12, C, LANES),
            vm(4, 3, C, LANES), vm(4, 3, C, LANES),
            vm(C, C, dtype=F32), vm(C, LANES, dtype=F32), dma(6),
            dma(), dma(), dma(), dma(), dma(2), dma(2), dma(2), dma(2),
            dma(6), dma(6), dma(4), dma(4), dma(3), dma(3), dma(4), dma(4), dma(4), dma(4),
        ],
        compiler_params=pltpu.CompilerParams(
            collective_id=0, has_side_effects=True, vmem_limit_bytes=58 * 1024 * 1024),
    )(volume, kernel, beta.reshape(1, C), gamma, cotangent)
    normalized, dvol, kg, gg, bg = pl.pallas_call(
        finish,
        out_shape=(
            jax.ShapeDtypeStruct(norm.shape, BF),
            jax.ShapeDtypeStruct(dvol.shape, BF),
            jax.ShapeDtypeStruct((C, 27 * C), F32),
            jax.ShapeDtypeStruct((C, C), F32),
            jax.ShapeDtypeStruct((1, C), F32),
        ),
        in_specs=[hbm] * 3,
        out_specs=(hbm,) * 5,
        scratch_shapes=[vm(2, 4, 3, C, LANES), vm(C, 27 * C, dtype=F32), vm(C, C, dtype=F32),
                        vm(1, C, dtype=F32), vm(1, C, NX, LANES), vm(8, C, NX, LANES), dma(11)],
        compiler_params=pltpu.CompilerParams(vmem_limit_bytes=58 * 1024 * 1024),
    )(norm, dvol, full)
    if groups > 1:
        kg, gg, bg = jax.tree.map(lambda a: a * 0.125, lax.psum((kg, gg, bg), "space"))
    return normalized, dvol, kg, gg, bg.reshape(C)


def solution(mesh):
    blocks = P(("dp", "space"), None, None, None)
    return jax.shard_map(
        shards,
        mesh=mesh,
        in_specs=(blocks, P(), P(), P(), blocks),
        out_specs=(blocks, blocks, P("dp", None), P("dp", None), P("dp")),
        check_vma=False,
    )
```

```python
import functools
import math

import jax
import jax.numpy as jnp
from jax import lax
from jax.experimental import pallas as pl
from jax.experimental.pallas import tpu as pltpu
from jax.sharding import PartitionSpec as P

BF = jnp.bfloat16
F32 = jnp.float32
C = 96
NX = 8
LANES = 128
SZ = 16
ROWS = 9 * C
DEPTH = 1024
MESH = pl.DeviceIdType.MESH


def taps_of(parity):
    return ((1, 0),) if parity == 0 else ((2, 0), (0, 1))


def row_of(ty, tz):
    return (ty * 3 + tz) * C


def tile(x):
    return pl.ds(x * LANES, LANES)


def body(groups, scale, vol_h, ker_h, beta_h, gamma_h, cot_h, norm_h, dvol_h, full_h,
         norm_o, dvol_o, full, out_sem, vol, ker, beta, gamma, cot, tmp, V, Yp, Zp, Yr, Zr, Cr, Kf, WB, Gs, up, S, GY, GZ, GYr, GZr, GCr,
         part, gslab, sendA, recvA, sendB, recvB, gacc, bacc, in_sem,
         ysend, yrecv, zsend, zrecv, csend, crecv, xsend, xrecv,
         asend, arecv, bsend, brecv, gsend, grecv, dsend, drecv, esend, erecv):
    idx = lax.axis_index("space")
    gx = idx // 8
    by = idx // 2 % 4
    bz = idx % 2
    base = gx * 8

    def dev(jy, jz):
        return {"space": base + jy * 2 + jz}

    loads = [pltpu.make_async_copy(vol_h.at[pl.ds(4 * i, 4)], vol.at[pl.ds(4 * i, 4)], in_sem.at[i])
             for i in range(2)]
    loads += [pltpu.make_async_copy(src, dst, in_sem.at[2 + i]) for i, (src, dst) in enumerate(
        ((ker_h, ker), (cot_h, cot), (gamma_h, gamma), (beta_h, beta)))]
    for load in loads:
        load.start()

    barrier = pltpu.get_barrier_semaphore()
    for k in range(1, 8):
        peer = base + (idx - base + k) % 8
        pl.semaphore_signal(barrier, inc=1, device_id={"space": peer}, device_id_type=MESH)
    if groups > 1:
        @pl.when(gx > 0)
        def _():
            pl.semaphore_signal(barrier, inc=1, device_id={"space": idx - 8}, device_id_type=MESH)

        @pl.when(gx < groups - 1)
        def _():
            pl.semaphore_signal(barrier, inc=1, device_id={"space": idx + 8}, device_id_type=MESH)

    lane = lax.broadcasted_iota(jnp.int32, (C, LANES), 1)
    lz = lane % SZ
    ly = lane // SZ

    def roll(value, shift):
        shift = shift % LANES
        return value if shift == 0 else pltpu.roll(value, shift, 1)

    def remote(src, dst, ss, rs, target):
        return pltpu.make_async_remote_copy(
            src_ref=src, dst_ref=dst, send_sem=ss, recv_sem=rs,
            device_id=target, device_id_type=MESH)

    def spread_in(parities, px, _):
        for py, pz in parities:
            r = row_of(1 + py, 1 + pz)
            tmp[...] = vol[px * 4 + py * 2 + pz].astype(F32).reshape(C * NX, LANES)
            ya = jnp.zeros((C, LANES), F32)
            za = jnp.zeros((C, LANES), F32)
            for x in range(NX):
                t = tmp[pl.ds(x, C, stride=NX), :]
                V[px, r:r + C, tile(x + 1)] = t.astype(BF)
                if py:
                    ya = jnp.where(ly == x, roll(t, x * SZ - 112), ya)
                if pz:
                    za = jnp.where(lz == x, roll(t, x - 15), za)
            if py:
                Yp[px, pz] = ya.astype(BF)
            if pz:
                Zp[px, py] = za.astype(BF)
        return 0

    loads[0].wait()
    loads[1].wait()
    lax.fori_loop(0, 2, functools.partial(spread_in, ((1, 1), (1, 0), (0, 1))), 0)

    pl.semaphore_wait(barrier, 7)
    if groups > 1:
        @pl.when(gx > 0)
        def _():
            pl.semaphore_wait(barrier, 1)

        @pl.when(gx < groups - 1)
        def _():
            pl.semaphore_wait(barrier, 1)

    y_copy = remote(Yp, Yr, ysend, yrecv, dev((by + 1) % 4, bz))
    z_copy = remote(Zp, Zr, zsend, zrecv, dev(by, 1 - bz))
    c_copy = [remote(Yp.at[px, 1], Cr.at[px], csend.at[px], crecv.at[px], dev((by + 1) % 4, 1 - bz))
              for px in range(2)]

    @pl.when(by < 3)
    def _():
        y_copy.start()

        @pl.when(bz == 0)
        def _():
            for c in c_copy:
                c.start()

    @pl.when(bz == 0)
    def _():
        z_copy.start()

    lax.fori_loop(0, 2, functools.partial(spread_in, ((0, 0),)), 0)
    for load in loads[2:]:
        load.wait()
    for tx in range(3):
        Kf[tx] = ker[:, tx * ROWS:(tx + 1) * ROWS]
    WB[...] = jnp.zeros_like(WB)
    for tx in range(3):
        for py in range(2):
            for pz in range(2):
                q = (py * 2 + pz) * C
                for ty, sy in taps_of(py):
                    for tz, sz in taps_of(pz):
                        t = tx * 9 + ty * 3 + tz
                        w = ker[:, t * C:(t + 1) * C].astype(F32)
                        v = (sy * 2 + sz) * LANES
                        WB[tx, q:q + C, v:v + C] = w.T.astype(BF)
    for v in range(4):
        Gs[v * LANES + C:(v + 1) * LANES, :] = jnp.zeros((LANES - C, 9 * LANES), BF)
    if groups == 1:
        Gs[:, 8 * LANES:] = jnp.zeros((4 * LANES, LANES), BF)
        V[1, :, 0:LANES] = jnp.zeros((DEPTH, LANES), BF)
    V[:, ROWS:, :] = jnp.zeros((2, DEPTH - ROWS, 9 * LANES), BF)
    tmp[...] = cot[0].astype(F32).reshape(C * NX, LANES)
    for x in range(NX):
        up[:, tile(x)] = tmp[pl.ds(x, C, stride=NX), :]
    gam = gamma[...]
    gam_b = gam.astype(BF)
    gam_t = gam.T.astype(BF)
    eye = (lax.broadcasted_iota(jnp.int32, (C, C), 0) == lax.broadcasted_iota(jnp.int32, (C, C), 1))
    beta_col = jnp.sum(jnp.where(eye, beta[...], 0.0), axis=1, keepdims=True)

    @pl.when(by > 0)
    def _():
        y_copy.wait_recv()

        @pl.when(bz == 1)
        def _():
            for c in c_copy:
                c.wait_recv()

    @pl.when(by == 0)
    def _():
        Yr[...] = jnp.zeros_like(Yr)

    @pl.when((by == 0) | (bz == 0))
    def _():
        Cr[...] = jnp.zeros_like(Cr)

    @pl.when(bz == 1)
    def _():
        z_copy.wait_recv()

    @pl.when(bz == 0)
    def _():
        Zr[...] = jnp.zeros_like(Zr)

    def shifted(px, _):
        y0 = Yr[px, 0].astype(F32)
        y1 = Yr[px, 1].astype(F32)
        z0 = Zr[px, 0].astype(F32)
        z1 = Zr[px, 1].astype(F32)
        yz = jnp.where(lz == 0, roll(Cr[px].astype(F32), -15), roll(y1, 1))
        for x in range(NX):
            def get(ty, tz):
                r = row_of(ty, tz)
                return V[px, r:r + C, tile(x + 1)].astype(F32)

            def put(ty, tz, value):
                r = row_of(ty, tz)
                V[px, r:r + C, tile(x + 1)] = value.astype(BF)

            put(1, 0, jnp.where(lz == 0, roll(z0, -x), roll(get(1, 2), 1)))
            put(0, 1, jnp.where(ly == 0, roll(y0, -SZ * x), roll(get(2, 1), SZ)))
            d = get(2, 2)
            t = jnp.where(lz == 0, roll(z1, -x), roll(d, 1))
            put(2, 0, t)
            put(0, 2, jnp.where(ly == 0, roll(y1, -SZ * x), roll(d, SZ)))
            put(0, 0, jnp.where(ly == 0, roll(yz, -SZ * x), roll(t, SZ)))
        return 0

    lax.fori_loop(0, 2, shifted, 0)

    if groups > 1:
        x_copy = remote(V.at[1, :, pl.ds(8 * LANES, LANES)], V.at[1, :, pl.ds(0, LANES)],
                        xsend.at[0], xrecv.at[0], {"space": (idx + 8) % (groups * 8)})

        @pl.when(gx < groups - 1)
        def _():
            x_copy.start()

        @pl.when(gx > 0)
        def _():
            x_copy.wait_recv()

        @pl.when(gx == 0)
        def _():
            V[1, :, 0:LANES] = jnp.zeros((DEPTH, LANES), BF)

    gacc[...] = jnp.zeros_like(gacc)
    bacc[...] = jnp.zeros_like(bacc)

    def forward(i, _):
        lo = pl.multiple_of(i * 256, 256)
        hi = pl.multiple_of(i * 256 + LANES, LANES)
        conv = jnp.dot(Kf[1], V[0, 0:ROWS, pl.ds(hi, 256)], preferred_element_type=F32)
        conv += jnp.dot(Kf[0], V[1, 0:ROWS, pl.ds(lo, 256)], preferred_element_type=F32)
        conv += jnp.dot(Kf[2], V[1, 0:ROWS, pl.ds(hi, 256)], preferred_element_type=F32)
        sq = conv * conv
        sq_b = sq.astype(BF)
        r = lax.rsqrt(beta_col + jnp.dot(gam_b, sq_b, preferred_element_type=F32))
        u = up[:, pl.ds(lo, 256)]
        normalized = conv * r
        weighted = -0.5 * u * conv * r * r * r
        w_b = weighted.astype(BF)
        coupled = jnp.dot(gam_t, w_b, preferred_element_type=F32)
        g = u * r + 2.0 * conv * coupled
        Gs[0:C, pl.ds(lo, 256)] = g.astype(BF)
        gacc[...] += lax.dot_general(w_b, sq_b, (((1,), (1,)), ((), ())), preferred_element_type=F32)
        bacc[...] += weighted[:, :LANES] + weighted[:, LANES:]
        for xx in range(2):
            tmp[pl.ds(i * 2 + xx, C, stride=NX), :] = normalized[:, xx * LANES:(xx + 1) * LANES]
        return 0

    lax.fori_loop(0, 4, forward, 0)
    norm_o[0] = tmp[...].reshape(C, NX, LANES).astype(BF)
    stores = [pltpu.make_async_copy(norm_o, norm_h, out_sem.at[0])]
    stores[0].start()

    ya = jnp.zeros((C, LANES), F32)
    za = jnp.zeros((C, LANES), F32)
    for x in range(NX):
        t = Gs[0:C, tile(x)].astype(F32)
        ya = jnp.where(ly == x, roll(t, x * SZ), ya)
        za = jnp.where(lz == x, roll(t, x), za)
    GY[...] = ya.astype(BF)
    GZ[...] = za.astype(BF)
    gy_copy = remote(GY, GYr, gsend.at[0], grecv.at[0], dev((by + 3) % 4, bz))
    gz_copy = remote(GZ, GZr, gsend.at[1], grecv.at[1], dev(by, 1 - bz))
    gc_copy = remote(GY, GCr, gsend.at[2], grecv.at[2], dev((by + 3) % 4, 1 - bz))

    @pl.when(by > 0)
    def _():
        gy_copy.start()

        @pl.when(bz == 1)
        def _():
            gc_copy.start()

    @pl.when(bz == 1)
    def _():
        gz_copy.start()

    nt = (((1,), (1,)), ((), ()))
    bsum = jnp.sum(bacc[...], axis=1, keepdims=True) * scale
    gslab[...] = jnp.concatenate(
        [gacc[...] * scale, jnp.broadcast_to(bsum, (C, LANES - C))], axis=1)

    def slabs(pair):
        tx = pair // 4
        row = pl.multiple_of(pair % 4 * 256, 256)
        first = pl.multiple_of((tx + 1) // 2 * LANES, LANES)
        k = lax.dot_general(Gs[0:C, 0:8 * LANES],
                            V[(tx + 1) % 2, pl.ds(row, 256), pl.ds(first, 8 * LANES)],
                            nt, preferred_element_type=F32) * scale
        return k[:, :LANES], k[:, LANES:] + jnp.where(pair == 11, gslab[...], 0.0)

    def a_copy(i):
        return remote(sendA.at[pl.ds(2 * i, 2)], recvA.at[pl.ds(2 * i, 2)], asend.at[i], arecv.at[i],
                      dev(by, 1 - bz))

    away = (by // 2 + 1) % 2

    def theirs(step, _):
        i = (step + 3 * away) % 6
        low, high = slabs((1 - bz) * 6 + i)
        sendA[2 * i] = low.astype(BF)
        sendA[2 * i + 1] = high.astype(BF)
        a_copy(i).start()
        return 0

    lax.fori_loop(0, 6, theirs, 0)

    def ours(i, _):
        low, high = slabs(bz * 6 + i)
        part[2 * i] = low
        part[2 * i + 1] = high
        return 0

    b_copy = []
    for step in range(2):
        half = (away + step) % 2
        lax.fori_loop(3 * half, 3 * half + 3, ours, 0)
        for i in range(3):
            a_copy(3 * half + i).wait()
        for to in ((2 * half, 2 * half + 1) if step == 0 else (2 * half + 1 - by % 2,)):
            k = (to + 4 - by) % 4
            for i in range(3):
                j = to * 3 + i
                sendB[k, i] = (part[j] + recvA[j].astype(F32)).astype(BF)
            b_copy.append(remote(sendB.at[k], recvB.at[k], bsend.at[k], brecv.at[k], dev(to, bz)))
            b_copy[-1].start()

    @pl.when(by < 3)
    def _():
        gy_copy.wait_recv()

        @pl.when(bz == 0)
        def _():
            gc_copy.wait_recv()

    @pl.when(bz == 0)
    def _():
        gz_copy.wait_recv()

    @pl.when(by == 3)
    def _():
        GYr[...] = jnp.zeros_like(GYr)

    @pl.when((by == 3) | (bz == 1))
    def _():
        GCr[...] = jnp.zeros_like(GCr)

    @pl.when(bz == 1)
    def _():
        GZr[...] = jnp.zeros_like(GZr)

    y = GYr[...].astype(F32)
    z = GZr[...].astype(F32)
    yz = jnp.where(lz == SZ - 1, roll(GCr[...].astype(F32), 15), roll(y, -1))
    for x in range(NX):
        g = Gs[0:C, tile(x)].astype(F32)
        t = jnp.where(lz == SZ - 1, roll(z, 15 - x), roll(g, -1))
        Gs[LANES:LANES + C, tile(x)] = t.astype(BF)
        Gs[2 * LANES:2 * LANES + C, tile(x)] = jnp.where(
            ly == 7, roll(y, 112 - SZ * x), roll(g, -SZ)).astype(BF)
        Gs[3 * LANES:3 * LANES + C, tile(x)] = jnp.where(
            ly == 7, roll(yz, 112 - SZ * x), roll(t, -SZ)).astype(BF)

    if groups > 1:
        h_copy = remote(Gs.at[:, pl.ds(0, LANES)], Gs.at[:, pl.ds(8 * LANES, LANES)],
                        xsend.at[1], xrecv.at[1], {"space": (idx + (groups - 1) * 8) % (groups * 8)})

        @pl.when(gx > 0)
        def _():
            h_copy.start()

        @pl.when(gx < groups - 1)
        def _():
            h_copy.wait_recv()

        @pl.when(gx == groups - 1)
        def _():
            Gs[:, 8 * LANES:] = jnp.zeros((4 * LANES, LANES), BF)

    def back(px):
        def step(i, _):
            lo = pl.multiple_of(i * 256, 256)
            hi = pl.multiple_of(i * 256 + LANES, LANES)
            if px == 0:
                res = jnp.dot(WB[1], Gs[:, pl.ds(lo, 256)], preferred_element_type=F32)
            else:
                res = jnp.dot(WB[2], Gs[:, pl.ds(lo, 256)], preferred_element_type=F32)
                res += jnp.dot(WB[0], Gs[:, pl.ds(hi, 256)], preferred_element_type=F32)
            for q in range(4):
                for xx in range(2):
                    S[pl.ds(q * C * NX + i * 2 + xx, C, stride=NX), :] = (
                        res[q * C:(q + 1) * C, xx * LANES:(xx + 1) * LANES])
            return 0

        lax.fori_loop(0, 4, step, 0)
        for q in range(4):
            dvol_o[px * 4 + q] = S[q * C * NX:(q + 1) * C * NX].reshape(C, NX, LANES).astype(BF)
        stores.append(pltpu.make_async_copy(
            dvol_o.at[pl.ds(4 * px, 4)], dvol_h.at[pl.ds(4 * px, 4)], out_sem.at[1 + px]))
        stores[-1].start()

    back(0)

    for c in b_copy:
        c.wait()
    for i in range(3):
        total = part[by * 3 + i] + recvA[by * 3 + i].astype(F32)
        for k in range(1, 4):
            total += recvB[k, i].astype(F32)
        full[bz, by, i] = total.astype(BF)
    d_copy = []
    for k in (2, 1, 3):
        to = (by + k) % 4
        d_copy.append(remote(full.at[bz, by], full.at[bz, by], dsend.at[k], drecv.at[k], dev(to, bz)))
        d_copy[-1].start()

    def e_copy(half, k):
        source = (by + 4 - k) % 4
        return remote(full.at[half, source], full.at[half, source], esend.at[k], erecv.at[k],
                      dev(by, 1 - bz))

    e_copy(bz, 0).start()

    back(1)

    for k in (1, 3, 2):
        source = (by + 4 - k) % 4
        remote(full.at[bz, source], full.at[bz, source], dsend.at[k], drecv.at[k],
               dev((by + k) % 4, bz)).wait_recv()
        e_copy(bz, k).start()
    for k in range(4):
        e_copy(1 - bz, k).wait_recv()
        e_copy(bz, k).wait_send()
    for d in d_copy:
        d.wait_send()

    stores.append(pltpu.make_async_copy(full, full_h, out_sem.at[3]))
    stores[-1].start()
    for store in stores:
        store.wait()

    @pl.when(by < 3)
    def _():
        y_copy.wait_send()

        @pl.when(bz == 0)
        def _():
            for c in c_copy:
                c.wait_send()

    @pl.when(bz == 0)
    def _():
        z_copy.wait_send()

    @pl.when(by > 0)
    def _():
        gy_copy.wait_send()

        @pl.when(bz == 1)
        def _():
            gc_copy.wait_send()

    @pl.when(bz == 1)
    def _():
        gz_copy.wait_send()

    if groups > 1:
        @pl.when(gx < groups - 1)
        def _():
            x_copy.wait_send()

        @pl.when(gx > 0)
        def _():
            h_copy.wait_send()


def finish(norm, dvol, full_h, norm_o, dvol_o, kg_o, gg_o, bg_o, full, kg, gg, bg, norm_v, dvol_v, sem):
    load = pltpu.make_async_copy(full_h, full, sem.at[5])
    load.start()
    fetch = [pltpu.make_async_copy(dvol.at[pl.ds(2 * i, 2)], dvol_v.at[pl.ds(2 * i, 2)], sem.at[6 + i])
             for i in range(4)]
    fetch.append(pltpu.make_async_copy(norm, norm_v, sem.at[10]))
    for f in fetch:
        f.start()
    copies = []
    load.wait()
    for tx in range(3):
        for s in range(7):
            j = tx * 8 + s
            n = min(LANES, ROWS - s * LANES)
            at = tx * ROWS + s * LANES
            kg[:, at:at + n] = full[j // 12, j % 12 // 3, j % 3][:, :n].astype(F32)
    copies.append(pltpu.make_async_copy(kg, kg_o, sem.at[2]))
    copies[-1].start()
    for i in range(4):
        fetch[i].wait()
        copies.append(pltpu.make_async_copy(
            dvol_v.at[pl.ds(2 * i, 2)], dvol_o.at[pl.ds(2 * i, 2)], sem.at[11 + i]))
        copies[-1].start()
    fetch[4].wait()
    copies.append(pltpu.make_async_copy(norm_v, norm_o, sem.at[1]))
    copies[-1].start()
    last = full[1, 3, 2].astype(F32)
    eye = (lax.broadcasted_iota(jnp.int32, (C, C), 0) == lax.broadcasted_iota(jnp.int32, (C, C), 1))
    gg[...] = last[:, :C]
    bg[...] = jnp.sum(jnp.where(eye, last[:, C:C + 1], 0.0), axis=0, keepdims=True)
    copies.append(pltpu.make_async_copy(gg, gg_o, sem.at[3]))
    copies.append(pltpu.make_async_copy(bg, bg_o, sem.at[4]))
    copies[-2].start()
    copies[-1].start()
    for c in copies:
        c.wait()


def shards(volume, kernel, beta, gamma, cotangent):
    devices = lax.axis_size("space")
    groups = devices // 8
    scale = 1.0 / math.sqrt(NX * LANES * devices)
    vm = lambda *shape, dtype=BF: pltpu.VMEM(shape, dtype)
    dma = lambda *shape: pltpu.SemaphoreType.DMA(shape) if shape else pltpu.SemaphoreType.DMA
    hbm = pl.BlockSpec(memory_space=pltpu.HBM)
    norm, dvol, full = pl.pallas_call(
        functools.partial(body, groups, scale),
        out_shape=(
            jax.ShapeDtypeStruct((1, C, NX, LANES), BF),
            jax.ShapeDtypeStruct((8, C, NX, LANES), BF),
            jax.ShapeDtypeStruct((2, 4, 3, C, LANES), BF),
        ),
        in_specs=[hbm] * 5,
        out_specs=(hbm,) * 3,
        scratch_shapes=[
            vm(1, C, NX, LANES), vm(8, C, NX, LANES), vm(2, 4, 3, C, LANES), dma(4),
            vm(8, C, NX, LANES), vm(C, 27 * C), vm(1, C, dtype=F32), vm(C, C, dtype=F32), vm(1, C, NX, LANES),
            vm(C * NX, LANES, dtype=F32), vm(2, DEPTH, 9 * LANES),
            vm(2, 2, C, LANES), vm(2, 2, C, LANES), vm(2, 2, C, LANES), vm(2, 2, C, LANES), vm(2, C, LANES),
            vm(3, C, ROWS), vm(3, 4 * C, 4 * LANES), vm(4 * LANES, 9 * LANES),
            vm(C, NX * LANES, dtype=F32), vm(4 * C * NX, LANES, dtype=F32),
            vm(C, LANES), vm(C, LANES), vm(C, LANES), vm(C, LANES), vm(C, LANES),
            vm(12, C, LANES, dtype=F32), vm(C, LANES, dtype=F32), vm(12, C, LANES), vm(12, C, LANES),
            vm(4, 3, C, LANES), vm(4, 3, C, LANES),
            vm(C, C, dtype=F32), vm(C, LANES, dtype=F32), dma(6),
            dma(), dma(), dma(), dma(), dma(2), dma(2), dma(2), dma(2),
            dma(6), dma(6), dma(4), dma(4), dma(3), dma(3), dma(4), dma(4), dma(4), dma(4),
        ],
        compiler_params=pltpu.CompilerParams(
            collective_id=0, has_side_effects=True, vmem_limit_bytes=58 * 1024 * 1024),
    )(volume, kernel, beta.reshape(1, C), gamma, cotangent)
    normalized, dvol, kg, gg, bg = pl.pallas_call(
        finish,
        out_shape=(
            jax.ShapeDtypeStruct(norm.shape, BF),
            jax.ShapeDtypeStruct(dvol.shape, BF),
            jax.ShapeDtypeStruct((C, 27 * C), F32),
            jax.ShapeDtypeStruct((C, C), F32),
            jax.ShapeDtypeStruct((1, C), F32),
        ),
        in_specs=[hbm] * 3,
        out_specs=(hbm,) * 5,
        scratch_shapes=[vm(2, 4, 3, C, LANES), vm(C, 27 * C, dtype=F32), vm(C, C, dtype=F32),
                        vm(1, C, dtype=F32), vm(1, C, NX, LANES), vm(8, C, NX, LANES), dma(15)],
        compiler_params=pltpu.CompilerParams(vmem_limit_bytes=58 * 1024 * 1024),
    )(norm, dvol, full)
    if groups > 1:
        kg, gg, bg = jax.tree.map(lambda a: a * 0.125, lax.psum((kg, gg, bg), "space"))
    return normalized, dvol, kg, gg, bg.reshape(C)


def solution(mesh):
    blocks = P(("dp", "space"), None, None, None)
    return jax.shard_map(
        shards,
        mesh=mesh,
        in_specs=(blocks, P(), P(), P(), blocks),
        out_specs=(blocks, blocks, P("dp", None), P("dp", None), P("dp")),
        check_vma=False,
    )
```
